32 devices in a mesh: gx: 2 (over x), gy: 4 (over y, core), gz: 4 (over z).
Axes of the slice: x: 2, y: 2, z: 4, core: 2. Of those that a mesh axis runs over, the one named last changes fastest.
Arguments:
- loads: float32 [16, 131072], P(None, ('gx', 'gy', 'gz')), may hold values from -50 to 50
- displacement: float32 [131072], P(('gx', 'gy', 'gz')), may hold values from -6 to 6
- stiffness: float32 [2048, 7, 4096], P(('gx', 'gy', 'gz')), may hold values from -100 to 300, as said below
- col_index: int32 [2048, 7], P(('gx', 'gy', 'gz')), may hold values from 0 to 159, as said below
- face_index: int32 [192, 16], P(('gx', 'gy', 'gz')), may hold values from 0 to 63, as said below
- zone_map: int32 [2048, 6], P(('gx', 'gy', 'gz')), may hold values from 0 to 4095, as said below
Outputs:
- adjoint: float32 [16, 131072], P(None, ('gx', 'gy', 'gz'))
- sensitivity: float32 [16, 4096], P(None, ('gx', 'gy', 'gz'))
The draws below stay inside these ranges and needn't reach their ends.
Inputs may be any that keep to these rules, and one draw needn't show every extreme that they name: `col_index`: in each aligned block of 64 rows (one subdomain), entry 0 of row r is r, and entries 1 to 6 name the row's coupled node blocks in directions -x, +x, -y, +y, -z, +z: one of the same subdomain by its row within the block, one across a face by 64 + d * 16 + f, f being the row's position in that subdomain's face list for direction d. Block at position f of a face in direction d touches the block at position f of the neighbour's face in the opposite direction. `face_index`: row 6 * s + d lists, each once, the subdomain's node blocks (rows within its block of 64) on its face in direction d. `zone_map`: entries of subdomain s lie in zones s * 128 to s * 128 + 2 * 128 - 1, taken modulo 4096; both ends of this window occur in every subdomain. `stiffness`: the whole operator is symmetric positive definite; diagonal entries of the diagonal blocks are positive.
All inputs are finite; a program needn't handle non-finite values.
Results may differ from the reference program's by a relative error of at most 0.0003.
Values sent between devices are 32-bit elements; how exact they have to be, the bound alone decides.
No kernel may reach another device: no remote copies, remote signals or barrier semaphores. Data moves between devices by JAX's collectives and lax.ppermute only.
A program may use at most 128 MiB of HBM per device.

```python
import jax
import jax.numpy as jnp
from jax import lax

BSIDE = 4
BDOF = 64
OUTS = 16
ITERS = 2
ZONE_DEV = 128
NBLK = 64
FACE = 16
SUB_X = 2
SUB_Y = 4
SUB_Z = 4
SUBDOMAINS = 32
BLOCKS = 2048
DOFS = 131072
ZONES = 4096


def subdomain_perms(key):
    base_key = jax.random.fold_in(key, 11)

    def one_perm(sub_id):
        return jax.random.permutation(jax.random.fold_in(base_key, sub_id), NBLK).astype(jnp.int32)
    return jax.vmap(one_perm)(jnp.arange(SUBDOMAINS, dtype=jnp.int32))


def grid_coords():
    cell_ids = jnp.arange(NBLK, dtype=jnp.int32)
    return (cell_ids // (BSIDE * BSIDE), cell_ids // BSIDE % BSIDE, cell_ids % BSIDE)


def neighbour_table(perm):
    first, second, third = grid_coords()
    coord_list = [first, second, third]
    face_pos = [second * BSIDE + third, first * BSIDE + third, first * BSIDE + second]
    columns = [perm]
    for direction in range(6):
        axis_id = direction // 2
        offset = 1 if direction % 2 == 1 else -1
        moved = [coord_list[0], coord_list[1], coord_list[2]]
        moved[axis_id] = moved[axis_id] + offset
        inside = (moved[axis_id] >= 0) & (moved[axis_id] < BSIDE)
        clipped = [jnp.clip(moved[0], 0, BSIDE - 1), jnp.clip(moved[1], 0, BSIDE - 1), jnp.clip(moved[2], 0, BSIDE - 1)]
        target = (clipped[0] * BSIDE + clipped[1]) * BSIDE + clipped[2]
        outside_id = NBLK + direction * FACE + face_pos[axis_id]
        columns.append(jnp.where(inside, perm[target], outside_id).astype(jnp.int32))
    table = jnp.stack(columns, axis=1)
    return jnp.zeros_like(table).at[perm].set(table)


def face_table(perm):
    spots = jnp.arange(FACE, dtype=jnp.int32)
    high_part = spots // BSIDE
    low_part = spots % BSIDE
    last = BSIDE - 1
    cells = jnp.stack([spots, last * FACE + spots, high_part * FACE + low_part, high_part * FACE + last * BSIDE + low_part, spots * BSIDE, spots * BSIDE + last], axis=0)
    return perm[cells]


def draw_col_index(key, part):
    perms = subdomain_perms(key)
    return jax.vmap(neighbour_table)(perms).reshape(BLOCKS, 7)


def draw_face_index(key, part):
    perms = subdomain_perms(key)
    return jax.vmap(face_table)(perms).reshape(SUBDOMAINS * 6, FACE)


def draw_stiffness(key, part):
    perms = subdomain_perms(key)
    edge_key = jax.random.fold_in(key, 23)
    node_key = jax.random.fold_in(key, 29)
    weight_lo, weight_hi, shift_lo, shift_hi = (0.25, 2.5, 0.3, 3.0)
    spans = [SUB_X * BSIDE + 1, SUB_Y * BSIDE + 1, SUB_Z * BSIDE + 1]

    def coupling(edge_id):
        inner_key = jax.random.fold_in(edge_key, edge_id)
        factor = jnp.clip(jax.random.normal(inner_key, (BDOF, BDOF), jnp.float32), -6.0, 6.0)
        weight = jnp.exp(jax.random.uniform(jax.random.fold_in(inner_key, 1), (), jnp.float32, jnp.log(weight_lo), jnp.log(weight_hi)))
        return weight * jnp.dot(factor, factor.T, precision=lax.Precision.HIGHEST) / BDOF

    def node_shift(node_id):
        return jnp.exp(jax.random.uniform(jax.random.fold_in(node_key, node_id), (BDOF,), jnp.float32, jnp.log(shift_lo), jnp.log(shift_hi)))

    def one_sub(pair):
        sub_id, perm = pair
        first, second, third = grid_coords()
        glob = [sub_id // (SUB_Y * SUB_Z) * BSIDE + first, sub_id // SUB_Z % SUB_Y * BSIDE + second, sub_id % SUB_Z * BSIDE + third]
        pieces = []
        for direction in range(6):
            axis_id = direction // 2
            edge_pos = [glob[0], glob[1], glob[2]]
            edge_pos[axis_id] = edge_pos[axis_id] + direction % 2
            edge_id = ((axis_id * spans[0] + edge_pos[0]) * spans[1] + edge_pos[1]) * spans[2] + edge_pos[2]
            pieces.append(jax.vmap(coupling)(edge_id.astype(jnp.int32)))
        couplings = jnp.stack(pieces, axis=1)
        node_id = (glob[0] * (SUB_Y * BSIDE) + glob[1]) * (SUB_Z * BSIDE) + glob[2]
        shifts = jax.vmap(node_shift)(node_id.astype(jnp.int32))
        diag_block = jax.vmap(jnp.diag)(shifts) + jnp.sum(couplings, axis=1)
        table = jnp.concatenate([diag_block[:, None], -couplings], axis=1).reshape(NBLK, 7, BDOF * BDOF)
        return jnp.zeros_like(table).at[perm].set(table)
    values = lax.map(one_sub, (jnp.arange(SUBDOMAINS, dtype=jnp.int32), perms))
    return values.reshape(BLOCKS, 7, BDOF * BDOF).astype(jnp.float32)


def draw_zone_map(key, part):
    width = NBLK * 6
    offsets = jax.random.randint(jax.random.fold_in(key, 31), (SUBDOMAINS, width), 0, 2 * ZONE_DEV, jnp.int32)
    high_spot = jax.random.randint(jax.random.fold_in(key, 37), (SUBDOMAINS,), 0, width, jnp.int32)
    gap_spot = jax.random.randint(jax.random.fold_in(key, 41), (SUBDOMAINS,), 1, width, jnp.int32)
    low_spot = (high_spot + gap_spot) % width
    sub_ids = jnp.arange(SUBDOMAINS, dtype=jnp.int32)
    offsets = offsets.at[sub_ids, high_spot].set(2 * ZONE_DEV - 1)
    offsets = offsets.at[sub_ids, low_spot].set(0)
    zones_all = (sub_ids[:, None] * ZONE_DEV + offsets) % ZONES
    return zones_all.reshape(BLOCKS, 6).astype(jnp.int32)


def draw_loads(key, part):
    sub_of = jnp.arange(DOFS, dtype=jnp.int32) // (NBLK * BDOF)
    sub_scale = jnp.exp(jnp.log(3.0) * sub_of.astype(jnp.float32) / (SUBDOMAINS - 1))
    col_scale = jnp.exp(jax.random.uniform(jax.random.fold_in(key, 2), (OUTS, 1), jnp.float32, 0.0, jnp.log(10.0))) / 3.0
    base = jnp.clip(jax.random.normal(jax.random.fold_in(key, 3), (OUTS, DOFS), jnp.float32), -5.0, 5.0)
    return (base * col_scale * sub_scale[None, :]).astype(jnp.float32)


def level_of(key, shape, split, least, high):
    level, own = 1.0, jax.random.fold_in(key, 6)
    for axis_at, blocks in split:
        heights = jnp.exp(jax.random.uniform(jax.random.fold_in(own, axis_at), (blocks,), jnp.float32, least / len(split), high / len(split)))
        level = level * jnp.repeat(heights, shape[axis_at] // blocks).reshape([-1 if axis == axis_at else 1 for axis in range(len(shape))])
    return level


def noise(own_key, dims, deviation, reach, split=(), kind=jnp.bfloat16):
    array = jax.random.normal(own_key, dims, jnp.float32) * deviation
    if len(split) > 0:
        array = level_of(own_key, dims, split, -0.22, 0.18) * array
    return jnp.clip(array, min=-reach, max=reach).astype(kind)


def setup_inputs(seed: int = 0) -> dict:
    key_of = jax.random.split(jax.random.key(seed), 7)
    return {
        "loads": draw_loads(jax.random.fold_in(key_of[6], 71), 0),
        "displacement": noise(key_of[1], (DOFS,), 1.0, 6.0, ((0, 32),), jnp.float32),
        "stiffness": draw_stiffness(jax.random.fold_in(key_of[6], 71), 0),
        "col_index": draw_col_index(jax.random.fold_in(key_of[6], 71), 0),
        "face_index": draw_face_index(jax.random.fold_in(key_of[6], 71), 0),
        "zone_map": draw_zone_map(jax.random.fold_in(key_of[6], 71), 0),
    }


def halo_from(grid_side, axis_id, from_low):
    pads = [(0, 0)] * grid_side.ndim
    pads[axis_id] = (1, 0) if from_low else (0, 1)
    padded = jnp.pad(grid_side, pads)
    begin = 0 if from_low else 1
    return lax.slice_in_dim(padded, begin, begin + grid_side.shape[axis_id], axis=axis_id)

def pick_faces(cube_in, face_list):
    return cube_in[:, face_list]

def pick_cols(extended, col_list):
    return extended[:, col_list]

def extend_all(field_in, face_index):
    height = field_in.shape[0]
    cubes = field_in.reshape(height, SUBDOMAINS, NBLK, BDOF).transpose(1, 0, 2, 3)
    lists = face_index.reshape(SUBDOMAINS, 6, FACE)
    picked = jax.vmap(pick_faces)(cubes, lists)
    grid = picked.reshape(SUB_X, SUB_Y, SUB_Z, height, 6, FACE, BDOF)
    sides = [halo_from(grid[:, :, :, :, 1], 0, True), halo_from(grid[:, :, :, :, 0], 0, False), halo_from(grid[:, :, :, :, 3], 1, True), halo_from(grid[:, :, :, :, 2], 1, False), halo_from(grid[:, :, :, :, 5], 2, True), halo_from(grid[:, :, :, :, 4], 2, False)]
    halos = jnp.stack(sides, axis=4).reshape(SUBDOMAINS, height, 6 * FACE, BDOF)
    return jnp.concatenate([cubes, halos], axis=2)

def apply_all(field_in, blocks, col_index, face_index):
    extended = extend_all(field_in, face_index)
    col_lists = col_index.reshape(SUBDOMAINS, NBLK, 7)
    gathered = jax.vmap(pick_cols)(extended, col_lists)
    image = jnp.einsum('nakij,ncakj->ncai', blocks, gathered, precision=lax.Precision.HIGHEST)
    return image.transpose(1, 0, 2, 3).reshape(field_in.shape[0], DOFS)

def inner_gram(left_in, right_in):
    return jnp.dot(left_in, right_in.T, precision=lax.Precision.HIGHEST)

def cho_apply(matrix_in, right_in):
    factor = jnp.linalg.cholesky(matrix_in)
    return jax.scipy.linalg.cho_solve((factor, True), right_in)

def reference(loads, displacement, stiffness, col_index, face_index, zone_map):
    blocks = stiffness.reshape(SUBDOMAINS, NBLK, 7, BDOF, BDOF)
    inverse_diag = (1.0 / jnp.diagonal(blocks[:, :, 0], axis1=2, axis2=3)).reshape(DOFS)
    adjoint = jnp.zeros_like(loads)
    residual = loads
    precond = residual * inverse_diag[None, :]
    direction = precond
    norm_gram = inner_gram(residual, precond)
    for step in range(ITERS):
        image = apply_all(direction, blocks, col_index, face_index)
        curvature = inner_gram(direction, image)
        step_size = cho_apply(curvature, norm_gram)
        adjoint = adjoint + jnp.dot(step_size.T, direction, precision=lax.Precision.HIGHEST)
        residual = residual - jnp.dot(step_size.T, image, precision=lax.Precision.HIGHEST)
        if step + 1 < ITERS:
            precond = residual * inverse_diag[None, :]
            next_gram = inner_gram(residual, precond)
            mix_ratio = cho_apply(norm_gram, next_gram)
            direction = precond + jnp.dot(mix_ratio.T, direction, precision=lax.Precision.HIGHEST)
            norm_gram = next_gram
    stacked = jnp.concatenate([adjoint, displacement[None, :]], axis=0)
    extended = extend_all(stacked, face_index)
    col_lists = col_index.reshape(SUBDOMAINS, NBLK, 7)
    beside = jax.vmap(pick_cols)(extended, col_lists[:, :, 1:])
    own_blocks = extended[:, :, :NBLK]
    differ = own_blocks[:, :, :, None, :] - beside
    moved = jnp.einsum('nakij,nakj->naki', blocks[:, :, 1:], differ[:, OUTS], precision=lax.Precision.HIGHEST)
    term = 0.5 * jnp.einsum('ncaki,naki->nakc', differ[:, :OUTS], moved, precision=lax.Precision.HIGHEST)
    term = term.reshape(BLOCKS * 6, OUTS)
    sensitivity = jax.ops.segment_sum(term, zone_map.reshape(-1), num_segments=ZONES).T
    return (adjoint, sensitivity)
```

```python
import functools

import jax
import jax.numpy as jnp
from jax import lax
from jax.experimental import pallas as pl
from jax.experimental.pallas import tpu as pltpu
from jax.sharding import PartitionSpec as P

AXES = ("gx", "gy", "gz")
F32 = jnp.float32
BF16 = jnp.bfloat16
NT = (((1,), (1,)), ((), ()))
VMEM_LIMIT = 16 * 1024 * 1024

NBLK = 64
BDOF = 64
OUTS = 16
FACE = 16
HALF = FACE // 2
EXTB = NBLK + 6 * FACE
COUPLED = 7
PAIRS = 4
WIDE = PAIRS * 2 * BDOF
DEPTH = 8
STEPS = NBLK // DEPTH
TILES = BDOF // 2
GROUP = 16
ROW_STRIDE = 3
BLOCK_STRIDE = ROW_STRIDE * TILES + 1
ZONE_DEV = 128
WINDOW = 2 * ZONE_DEV


def spec_smem():
    return pl.BlockSpec(memory_space=pltpu.SMEM)


def spec_full(shape):
    return pl.BlockSpec(shape, lambda *_: (0,) * len(shape))


def spec_vmem():
    return pl.BlockSpec(memory_space=pltpu.VMEM)


def in_vmem(value):
    return pltpu.with_memory_space_constraint(value, pltpu.VMEM)


def in_hbm(value):
    return pltpu.with_memory_space_constraint(value, pltpu.HBM)


def params(flops, moved):
    return dict(
        compiler_params=pltpu.CompilerParams(vmem_limit_bytes=VMEM_LIMIT),
        cost_estimate=pl.CostEstimate(flops=flops, bytes_accessed=moved, transcendentals=0),
    )


def lanes(shape):
    return lax.broadcasted_iota(jnp.int32, shape, len(shape) - 1)


def low_half(shape):
    return lanes(shape) < BDOF


def swap_halves(value):
    return pltpu.roll(value, BDOF, value.ndim - 1)


def split_pair(tile):
    low = low_half(tile.shape)
    other = swap_halves(tile)
    return jnp.where(low, tile, other), jnp.where(low, other, tile)


def join_pair(first, second):
    return jnp.where(low_half(first.shape), first, second)


def high_low(value):
    high = value.astype(BF16)
    low = (value - high.astype(F32)).astype(BF16)
    return jnp.concatenate([high, low], axis=0)


def fold_rows(value):
    half = value.shape[0] // 2
    return value[:half] + value[half:]


def interleave(value):
    high = value.astype(BF16).astype(F32)
    rest = value - high
    middle = rest.astype(BF16).astype(F32)
    lowest = rest - middle
    low = low_half(value.shape)
    parts = jnp.concatenate([jnp.where(low, high, middle), lowest], axis=1).astype(BF16)
    source = lax.broadcasted_iota(jnp.int32, (4 * BDOF, 2 * BDOF), 0)
    target = lanes((4 * BDOF, 2 * BDOF)) % BDOF
    within = source % BDOF
    place = (within % (BDOF // 2)) * 2 + within // (BDOF // 2)
    mover = jnp.where((place == target) & (source < 3 * BDOF), 1.0, 0.0).astype(BF16)
    return jnp.dot(parts, mover, preferred_element_type=F32)


def slots_of(sizes):
    order = []
    for axis in (2, 0, 1):
        for turn in (0, 1) if axis == 2 else (1, 0):
            if sizes[axis] > 1 + turn:
                order.append((axis, turn))
    return order


def side_of(slot):
    axis, turn = slot
    odd = lax.axis_index(AXES[axis]) % 2
    return 2 * axis + (odd if turn else 1 - odd)


def partner_exists(slot, sizes):
    axis, turn = slot
    place = lax.axis_index(AXES[axis])
    partner = place + 2 * (side_of(slot) % 2) - 1
    return (partner >= 0) & (partner < sizes[axis])


def start_kernel(slots, face_ref, loads_ref, disp_ref, stiff_ref, dirs_ref, inv_ref, *rest):
    msgs, (udup_ref,) = rest[:-1], rest[-1:]
    lane = lanes((DEPTH, 2 * BDOF))
    for step in range(STEPS):
        rows = slice(step * DEPTH, (step + 1) * DEPTH)
        parts = []
        for tile in range(TILES):
            part = stiff_ref[0, rows, tile * 128:(tile + 1) * 128]
            parts.append(jnp.where((lane == 2 * tile) | (lane == BDOF + 2 * tile + 1), part, 0.0))
        while len(parts) > 1:
            parts = [one + two for one, two in zip(parts[::2], parts[1::2])]
        inv_ref[rows, :] = 1.0 / (parts[0] + swap_halves(parts[0]))
    for pair in range(NBLK // 2):
        first, second = split_pair(loads_ref[:, pair * 128:(pair + 1) * 128])
        dirs_ref[2 * pair] = first * inv_ref[2 * pair:2 * pair + 1, :]
        dirs_ref[2 * pair + 1] = second * inv_ref[2 * pair + 1:2 * pair + 2, :]
    one, two = split_pair(disp_ref[...])
    udup_ref[pl.ds(0, NBLK // 2, stride=2), :] = one
    udup_ref[pl.ds(1, NBLK // 2, stride=2), :] = two
    for msg, slot in zip(msgs, slots):
        side = side_of(slot)
        for pair in range(HALF):
            one, two = face_ref[side, 2 * pair], face_ref[side, 2 * pair + 1]
            msg[pair * OUTS:(pair + 1) * OUTS, :] = join_pair(dirs_ref[one], dirs_ref[two])
            msg[HALF * OUTS + pair:HALF * OUTS + pair + 1, :] = join_pair(
                udup_ref[pl.ds(one, 1), :], udup_ref[pl.ds(two, 1), :]
            )


def start(slots, face_index, loads, disp, stiffness):
    msg_rows = HALF * (OUTS + 1)
    outs = [
        jax.ShapeDtypeStruct((NBLK, OUTS, 2 * BDOF), F32),
        jax.ShapeDtypeStruct((NBLK, 2 * BDOF), F32),
    ] + [jax.ShapeDtypeStruct((msg_rows, 2 * BDOF), F32)] * len(slots)
    return pl.pallas_call(
        functools.partial(start_kernel, slots),
        grid=(1,),
        in_specs=[
            spec_smem(),
            spec_full(loads.shape),
            spec_full(disp.shape),
            pl.BlockSpec((1, NBLK, BDOF * BDOF), lambda s: (0, 0, 0)),
        ],
        out_specs=[spec_full(o.shape) for o in outs],
        out_shape=outs,
        scratch_shapes=[pltpu.VMEM((NBLK, 2 * BDOF), F32)],
        name="start",
        **params(1 << 20, 2 << 20),
    )(face_index, in_hbm(loads), in_hbm(disp), in_hbm(stiffness))


def pack_kernel(stiff_ref, out_ref, block_ref, rows_ref, sems):
    span = DEPTH * BLOCK_STRIDE

    def copy(step):
        return pltpu.make_async_copy(
            stiff_ref.at[:, pl.ds(step * DEPTH, DEPTH), :], block_ref.at[step], sems.at[step]
        )

    for step in range(STEPS):
        copy(step).start()

    def chunk(step, carry):
        copy(step).wait()
        for side in range(COUPLED):
            for tile in range(TILES):
                rows_ref[pl.ds(side * span + tile * ROW_STRIDE, DEPTH, stride=BLOCK_STRIDE), :] = block_ref[
                    step, side, :, tile * 128:(tile + 1) * 128
                ]

        def matrix(side, row):
            return rows_ref[pl.ds(side * span + row * BLOCK_STRIDE, TILES, stride=ROW_STRIDE), :]

        for row in range(DEPTH):
            at = step * DEPTH + row
            for pair in range(PAIRS):
                first = matrix(2 * pair, row)
                second = matrix(2 * pair + 1, row) if 2 * pair + 1 < COUPLED else jnp.zeros_like(first)
                low = low_half(first.shape)
                even = jnp.where(low, first, swap_halves(second))
                odd = jnp.where(low, swap_halves(first), second)
                both = jnp.concatenate([even, odd], axis=0)
                out_ref[at, :, pair * 128:(pair + 1) * 128] = high_low(both)
        return carry

    lax.fori_loop(0, STEPS, chunk, 0)


def pack(stiffness):
    return pl.pallas_call(
        pack_kernel,
        in_specs=[pl.BlockSpec(memory_space=pltpu.HBM)],
        out_specs=spec_vmem(),
        out_shape=pltpu.VMEM((NBLK, 2 * BDOF, WIDE), BF16),
        scratch_shapes=[
            pltpu.VMEM((STEPS, COUPLED, DEPTH, BDOF * BDOF), F32),
            pltpu.VMEM((COUPLED * DEPTH * BLOCK_STRIDE + 8, 2 * BDOF), F32),
            pltpu.SemaphoreType.DMA((STEPS,)),
        ],
        name="pack",
        **params(1 << 24, 16 << 20),
    )(in_hbm(stiffness))


def two_parts(value):
    high = value.astype(BF16)
    return high, (value - high.astype(F32)).astype(BF16)


def fill_halos(store, slots, sizes, halos, first_row, rows):
    met = set()
    for slot, halo in zip(slots, halos):
        side = side_of(slot)
        met.add(slot)
        exists = None
        if slot[1] == 1 or sizes[slot[0]] % 2 == 1:
            exists = partner_exists(slot, sizes)
        for pair in range(HALF):
            at = NBLK + side * FACE + 2 * pair
            for extra, value in enumerate(split_pair(halo[first_row + pair * rows:first_row + (pair + 1) * rows, :])):
                store(at + extra, value if exists is None else jnp.where(exists, value, 0.0))
    for axis in range(3):
        for turn in range(2):
            if (axis, turn) not in met:
                side = side_of((axis, turn))
                for block in range(FACE):
                    store(NBLK + side * FACE + block, jnp.zeros((rows, 2 * BDOF), F32))


def fill_extended(slots, sizes, ext_ref, own_ref, halos):
    for block in range(NBLK):
        ext_ref[block] = high_low(own_ref[block])

    def store(at, value):
        ext_ref[at] = high_low(value)

    fill_halos(store, slots, sizes, halos, 0, OUTS)


def gathered(ext_ref, col_ref, row):
    pieces = []
    for pair in range(PAIRS):
        first = ext_ref[col_ref[2 * pair, row]]
        if 2 * pair + 1 < COUPLED:
            pieces.append(join_pair(first, ext_ref[col_ref[2 * pair + 1, row]]))
        else:
            pieces.append(join_pair(first, jnp.zeros_like(first)))
    return jnp.concatenate(pieces, axis=1)


def times_packed(field, packed):
    out = fold_rows(lax.dot_general(field, packed, NT, preferred_element_type=F32))
    return out + swap_halves(out)


def operate(col_ref, packed_ref, ext_ref, image_ref):
    def chunk(step, carry):
        for local in range(GROUP):
            row = step * GROUP + local
            at = pl.multiple_of(row * OUTS, OUTS)
            image_ref[pl.ds(at, OUTS), :] = times_packed(gathered(ext_ref, col_ref, row), packed_ref[row])
        return carry

    lax.fori_loop(0, NBLK // GROUP, chunk, 0)


def first_kernel(slots, sizes, col_ref, face_ref, packed_ref, dirs_ref, inv_ref, loads_ref, *rest):
    many = len(slots)
    halos, (w_ref, gram_ref), msgs = rest[:many], rest[many:many + 2], rest[many + 2:2 * many + 2]
    ext_ref, image_ref, left_ref, right_ref = rest[2 * many + 2:]
    fill_extended(slots, sizes, ext_ref, dirs_ref, halos)
    operate(col_ref, packed_ref, ext_ref, image_ref)
    image = interleave(image_ref[...])
    for pair in range(NBLK // 2):
        one = image[2 * pair * OUTS:(2 * pair + 1) * OUTS]
        two = image[(2 * pair + 1) * OUTS:(2 * pair + 2) * OUTS]
        w_one = one * inv_ref[2 * pair:2 * pair + 1, :]
        w_two = two * inv_ref[2 * pair + 1:2 * pair + 2, :]
        w_ref[2 * pair] = w_one
        w_ref[2 * pair + 1] = w_two
        at = slice(pair * 128, (pair + 1) * 128)
        own = join_pair(dirs_ref[2 * pair], dirs_ref[2 * pair + 1])
        left_ref[:, at] = high_low(
            jnp.concatenate([loads_ref[:, at], own, join_pair(w_one, w_two)], axis=0)
        )
        right_ref[:, at] = high_low(jnp.concatenate([own, join_pair(one, two)], axis=0))
    for msg, slot in zip(msgs, slots):
        side = side_of(slot)
        for pair in range(HALF):
            msg[pair * OUTS:(pair + 1) * OUTS, :] = join_pair(
                w_ref[face_ref[side, 2 * pair]], w_ref[face_ref[side, 2 * pair + 1]]
            )
    gram = fold_rows(lax.dot_general(left_ref[...], right_ref[...], NT, preferred_element_type=F32))
    gram = gram[:, :2 * OUTS] + gram[:, 2 * OUTS:]
    gram_ref[...] = jnp.concatenate(
        [gram[:OUTS, :OUTS], gram[OUTS:2 * OUTS, OUTS:], gram[2 * OUTS:, OUTS:]], axis=1
    )


def first(slots, sizes, col_index, face_index, packed, dirs, inv, loads, halos):
    outs = [
        jax.ShapeDtypeStruct((NBLK, OUTS, 2 * BDOF), F32),
        jax.ShapeDtypeStruct((OUTS, 3 * OUTS), F32),
    ] + [jax.ShapeDtypeStruct((HALF * OUTS, 2 * BDOF), F32)] * len(slots)
    return pl.pallas_call(
        functools.partial(first_kernel, slots, sizes),
        in_specs=[
            spec_smem(),
            spec_smem(),
            spec_vmem(),
            spec_full(dirs.shape),
            spec_full(inv.shape),
            spec_full(loads.shape),
        ] + [spec_full(h.shape) for h in halos],
        out_specs=[spec_full(o.shape) for o in outs],
        out_shape=outs,
        scratch_shapes=[
            pltpu.VMEM((EXTB, 2 * OUTS, 2 * BDOF), BF16),
            pltpu.VMEM((NBLK * OUTS, 2 * BDOF), F32),
            pltpu.VMEM((6 * OUTS, NBLK * BDOF), BF16),
            pltpu.VMEM((4 * OUTS, NBLK * BDOF), BF16),
        ],
        name="first",
        **params(1 << 28, 11 << 20),
    )(col_index, face_index, in_vmem(packed), dirs, inv, loads, *halos)


def second_kernel(slots, sizes, col_ref, packed_ref, w_ref, early_ref, after_ref, *rest):
    del after_ref
    many = len(slots)
    halos, (gram_ref, ext_ref, image_ref, left_ref, right_ref) = rest[:many], rest[many:]
    fill_extended(slots, sizes, ext_ref, w_ref, halos)
    operate(col_ref, packed_ref, ext_ref, image_ref)
    image = interleave(image_ref[...])
    for pair in range(NBLK // 2):
        one = image[2 * pair * OUTS:(2 * pair + 1) * OUTS]
        two = image[(2 * pair + 1) * OUTS:(2 * pair + 2) * OUTS]
        at = slice(pair * 128, (pair + 1) * 128)
        left_ref[:, at] = high_low(join_pair(w_ref[2 * pair], w_ref[2 * pair + 1]))
        right_ref[:, at] = high_low(join_pair(one, two))
    gram = fold_rows(lax.dot_general(left_ref[...], right_ref[...], NT, preferred_element_type=F32))
    grams = jnp.concatenate([gram[:, :OUTS] + gram[:, OUTS:], early_ref[...]], axis=1)
    tile = jnp.concatenate([grams[:8], grams[8:]], axis=1)
    for place in range(gram_ref.shape[0] // 8):
        gram_ref[place * 8:(place + 1) * 8, :] = tile


def second(slots, sizes, col_index, packed, w, early, after, halos):
    copies = sizes[0] * sizes[1] * sizes[2]
    return pl.pallas_call(
        functools.partial(second_kernel, slots, sizes),
        in_specs=[
            spec_smem(),
            spec_vmem(),
            spec_full(w.shape),
            spec_full(early.shape),
            pl.BlockSpec(memory_space=pl.ANY),
        ] + [spec_full(h.shape) for h in halos],
        out_specs=spec_full((copies * 8, 128)),
        out_shape=jax.ShapeDtypeStruct((copies * 8, 128), F32),
        scratch_shapes=[
            pltpu.VMEM((EXTB, 2 * OUTS, 2 * BDOF), BF16),
            pltpu.VMEM((NBLK * OUTS, 2 * BDOF), F32),
            pltpu.VMEM((2 * OUTS, NBLK * BDOF), BF16),
            pltpu.VMEM((2 * OUTS, NBLK * BDOF), BF16),
        ],
        name="second",
        **params(1 << 28, 11 << 20),
    )(col_index, in_vmem(packed), w, early, after, *halos)


def moved_kernel(slots, sizes, col_ref, packed_ref, disp_ref, *rest):
    many = len(slots)
    halos, (out_ref, udup_ref, near_ref, raw_ref) = rest[:many], rest[many:]
    one, two = split_pair(disp_ref[...])
    udup_ref[pl.ds(0, NBLK // 2, stride=2), :] = one
    udup_ref[pl.ds(1, NBLK // 2, stride=2), :] = two

    def store(at, value):
        udup_ref[pl.ds(at, 1), :] = value

    fill_halos(store, slots, sizes, halos, HALF * OUTS, 1)
    side_at = lax.broadcasted_iota(jnp.int32, (8, 128), 0)
    low = low_half((8, 128))

    def chunk(step, carry):
        for local in range(GROUP):
            row = step * GROUP + local
            own = udup_ref[pl.ds(row, 1), :]
            for side in range(COUPLED):
                near_ref[local * 8 + side:local * 8 + side + 1, :] = udup_ref[pl.ds(col_ref[side, row], 1), :]
            near_ref[local * 8 + 7:local * 8 + 8, :] = own
            differ = own - near_ref[local * 8:(local + 1) * 8, :]
            parts = []
            for pair in range(PAIRS):
                keep = ((side_at == 2 * pair) & low) | ((side_at == 2 * pair + 1) & ~low)
                part = jnp.where(keep, differ, 0.0)
                high = part.astype(BF16).astype(F32)
                parts.append(jnp.concatenate([high, part - high], axis=0).astype(BF16))
            field = jnp.concatenate(parts, axis=1)
            raw_ref[pl.ds(pl.multiple_of(row * 8, 8), 8), :] = times_packed(field, packed_ref[row])
        return carry

    lax.fori_loop(0, NBLK // GROUP, chunk, 0)
    out_ref[...] = interleave(raw_ref[...])


def moved(slots, sizes, col_index, packed, disp, halos):
    return pl.pallas_call(
        functools.partial(moved_kernel, slots, sizes),
        in_specs=[
            spec_smem(),
            spec_vmem(),
            spec_full(disp.shape),
        ] + [spec_full(h.shape) for h in halos],
        out_specs=spec_full((NBLK * 8, 128)),
        out_shape=jax.ShapeDtypeStruct((NBLK * 8, 128), F32),
        scratch_shapes=[
            pltpu.VMEM((EXTB, 2 * BDOF), F32),
            pltpu.VMEM((GROUP * 8, 2 * BDOF), F32),
            pltpu.VMEM((NBLK * 8, 2 * BDOF), F32),
        ],
        name="moved",
        **params(1 << 27, 10 << 20),
    )(col_index, in_vmem(packed), disp, *halos)


def terms_kernel(slots, sizes, col_ref, moved_ref, zone_ref, own_field_ref, *rest):
    many = len(slots)
    halos, (own_ref, sent_ref, field_ref, ext_ref, term_ref) = rest[:many], rest[-5:]
    before = rest[many:-5]
    fill_extended(slots, sizes, ext_ref, own_field_ref, halos)
    for pair in range(NBLK // 2):
        at = slice(pair * 128, (pair + 1) * 128)
        field_ref[:, at] = high_low(join_pair(own_field_ref[2 * pair], own_field_ref[2 * pair + 1]))
    side_at = lax.broadcasted_iota(jnp.int32, (8, 128), 0)
    low = low_half((8, 128))

    def chunk(step, carry):
        for local in range(GROUP):
            row = step * GROUP + local
            at = pl.multiple_of(row * 8, 8)
            value = moved_ref[pl.ds(at, 8), :]
            pieces = []
            for pair in range(PAIRS):
                drop = ((side_at == 2 * pair) & low) | ((side_at == 2 * pair + 1) & ~low)
                part = jnp.where(drop, -value, 0.0)
                if pair == 0:
                    part = jnp.where(low, value, part)
                high = part.astype(BF16).astype(F32)
                pieces.append(jnp.concatenate([high, part - high], axis=0).astype(BF16))
            fields = gathered(ext_ref, col_ref, row)
            out = lax.dot_general(
                jnp.concatenate(pieces, axis=1), fields, NT, preferred_element_type=F32
            )
            term_ref[pl.ds(at, 8), :2 * OUTS] = fold_rows(out)
        return carry

    lax.fori_loop(0, NBLK // GROUP, chunk, 0)
    across = jnp.concatenate([term_ref[pl.ds(side, NBLK, stride=8), :] for side in range(1, COUPLED)], axis=0)
    term = fold_rows(jnp.transpose(across)[:2 * OUTS])
    high = term.astype(BF16)
    rest_of = term - high.astype(F32)
    middle = rest_of.astype(BF16)
    stack = jnp.concatenate([high, middle, (rest_of - middle.astype(F32)).astype(BF16)], axis=0)
    me = (lax.axis_index(AXES[0]) * sizes[1] + lax.axis_index(AXES[1])) * sizes[2] + lax.axis_index(AXES[2])
    relative = zone_ref[...] - me * ZONE_DEV
    relative = jnp.where(relative < 0, relative + ZONE_DEV * sizes[0] * sizes[1] * sizes[2], relative)
    relative = jnp.concatenate([relative[side:side + 1, :] for side in range(COUPLED - 1)], axis=1)
    place = lax.broadcasted_iota(jnp.int32, (WINDOW, NBLK * (COUPLED - 1)), 0)
    member = jnp.where(relative == place, 1.0, 0.0).astype(BF16)
    sums = lax.dot_general(stack, member, NT, preferred_element_type=F32)
    sums = sums[:OUTS] + sums[OUTS:2 * OUTS] + sums[2 * OUTS:]
    for out_ref, part in ((own_ref, sums[:, :ZONE_DEV]), (sent_ref, sums[:, ZONE_DEV:])):
        out_ref[out_ref.shape[0] - OUTS:, :] = part
    for out_ref, earlier in zip((own_ref, sent_ref), before):
        out_ref[:OUTS, :] = earlier[...]


def terms(slots, sizes, col_index, values, zones, field, halos, before=()):
    operands = (values, zones, field, *halos, *before)
    rows = OUTS * (2 if before else 1)
    outs = [jax.ShapeDtypeStruct((rows, ZONE_DEV), F32)] * 2 + [
        jax.ShapeDtypeStruct((2 * OUTS, NBLK * BDOF), BF16)
    ]
    return pl.pallas_call(
        functools.partial(terms_kernel, slots, sizes),
        grid=(1,),
        in_specs=[spec_smem()] + [spec_full(o.shape) for o in operands],
        out_specs=[spec_full(o.shape) for o in outs],
        out_shape=outs,
        scratch_shapes=[
            pltpu.VMEM((EXTB, 2 * OUTS, 2 * BDOF), BF16),
            pltpu.VMEM((NBLK * 8, 128), F32),
        ],
        name="terms",
        **params(1 << 27, 4 << 20),
    )(col_index, *operands)


def times(left, right):
    parts = [left[:, i:i + 1] * right[i:i + 1, :] for i in range(left.shape[1])]
    while len(parts) > 1:
        parts = [one + two for one, two in zip(parts[::2], parts[1::2])]
    return parts[0]


def solve_spd(matrix, right):
    work = jnp.concatenate([matrix, right], axis=1)
    rows = lax.broadcasted_iota(jnp.int32, work.shape, 0)
    for at in range(0, OUTS, 2):
        first_col = jnp.broadcast_to(work[:, at:at + 1], work.shape)
        second_col = jnp.broadcast_to(work[:, at + 1:at + 2], work.shape)
        one, two = work[at:at + 1, :], work[at + 1:at + 2, :]
        top, side, end = first_col[at:at + 1], first_col[at + 1:at + 2], second_col[at + 1:at + 2]
        scale = 1.0 / (top * end - side * side)
        new_one = (end * one - side * two) * scale
        new_two = (top * two - side * one) * scale
        others = work - first_col * new_one - second_col * new_two
        work = jnp.where(rows == at, new_one, jnp.where(rows == at + 1, new_two, others))
    return work[:, OUTS:]


def finish_kernel(grams_ref, dirs_ref, w_ref, adj_ref, factors_ref):
    count = grams_ref.shape[0] // 8
    parts = [grams_ref[i * 8:(i + 1) * 8, :] for i in range(count)]
    while len(parts) > 1:
        parts = [sum(parts[i:i + 2][1:], parts[i]) for i in range(0, len(parts), 2)]
    gram = jnp.concatenate([parts[0][:, :4 * OUTS], parts[0][:, 4 * OUTS:]], axis=0)
    f_gram = gram[:, :OUTS]
    n_gram = gram[:, OUTS:2 * OUTS]
    c_gram = gram[:, 2 * OUTS:3 * OUTS]
    e_gram = gram[:, 3 * OUTS:]
    eye = jnp.where(
        lax.broadcasted_iota(jnp.int32, (OUTS, OUTS), 0) == lanes((OUTS, OUTS)), 1.0, 0.0
    )
    n_inverse = solve_spd(n_gram, eye)
    alpha = solve_spd(c_gram, n_gram)
    alpha_t = jnp.transpose(alpha)
    c_alpha = times(c_gram, alpha)
    e_alpha = times(e_gram, alpha)
    f_alpha = times(f_gram, alpha)
    next_gram = n_gram - c_alpha - jnp.transpose(c_alpha) + times(alpha_t, e_alpha)
    mixed = eye + times(n_inverse, next_gram)
    mixed_t = jnp.transpose(mixed)
    cross = times(mixed_t, e_alpha)
    curvature = times(mixed_t, times(c_gram, mixed)) - cross - jnp.transpose(cross) + times(alpha_t, f_alpha)
    beta_t = jnp.transpose(solve_spd(curvature, next_gram))
    on_dirs = alpha_t + times(beta_t, mixed_t)
    on_w = -times(beta_t, alpha_t)
    factors = jnp.concatenate([on_dirs, on_w], axis=1)
    high, low = two_parts(factors)
    factors_split = [high[:, :OUTS], high[:, :OUTS], high[:, OUTS:], high[:, OUTS:], low]
    dirs, w = dirs_ref[...], w_ref[...]
    adj_ref[...] = jnp.dot(
        jnp.concatenate(factors_split, axis=1),
        jnp.concatenate([dirs, w, dirs[:OUTS], w[:OUTS]], axis=0),
        preferred_element_type=F32,
    )
    factors_ref[...] = factors


def blend_kernel(factors_ref, own_ref, came_ref, sens_ref):
    sens_ref[...] = 0.5 * jnp.dot(
        factors_ref[...], own_ref[...] + came_ref[...], precision=lax.Precision.HIGHEST, preferred_element_type=F32
    )


def finish(grams, dirs, w):
    operands = (grams, dirs, w)
    outs = [
        jax.ShapeDtypeStruct((OUTS, NBLK * BDOF), F32),
        jax.ShapeDtypeStruct((OUTS, 2 * OUTS), F32),
    ]
    return pl.pallas_call(
        finish_kernel,
        in_specs=[spec_full(grams.shape), spec_vmem(), spec_vmem()],
        out_specs=[spec_full(o.shape) for o in outs],
        out_shape=outs,
        name="finish",
        **params(1 << 25, 8 << 20),
    )(grams, in_vmem(dirs), in_vmem(w))


def blend(factors, own, came):
    operands = (factors, own, came)
    return pl.pallas_call(
        blend_kernel,
        in_specs=[spec_full(o.shape) for o in operands],
        out_specs=spec_full((OUTS, ZONE_DEV)),
        out_shape=jax.ShapeDtypeStruct((OUTS, ZONE_DEV), F32),
        name="blend",
        **params(1 << 17, 1 << 16),
    )(*operands)


def exchange(slots, msgs):
    halos = []
    for (axis, turn), msg in zip(slots, msgs):
        count = lax.axis_size(AXES[axis])
        pairs = []
        for place in range(count):
            partner = place + 1 if place % 2 == turn else place - 1
            pairs.append((place, partner if 0 <= partner < count else place))
        halos.append(lax.ppermute(msg, AXES[axis], pairs))
    return halos


def on_device(loads, displacement, stiffness, col_index, face_index, zone_map):
    sizes = [lax.axis_size(axis) for axis in AXES]
    slots = slots_of(sizes)
    disp = displacement.reshape(NBLK // 2, 2 * BDOF)
    stiffness = jnp.swapaxes(stiffness, 0, 1)
    col_index = col_index.T
    dirs, inv, *msgs = start(slots, face_index, loads, disp, stiffness)
    halos_d = exchange(slots, msgs)
    packed = pack(stiffness)
    w, early, *msgs = first(slots, sizes, col_index, face_index, packed, dirs, inv, loads, halos_d)
    halos_w = exchange(slots, msgs)
    values = moved(slots, sizes, col_index, packed, disp, halos_d)
    count = lax.axis_size(AXES)
    zones = zone_map.T
    own, sent, field_d = terms(slots, sizes, col_index, values, zones, dirs, halos_d)
    grams = second(slots, sizes, col_index, packed, w, early, sent, halos_w)
    own, sent, field_w = terms(slots, sizes, col_index, values, zones, w, halos_w, (own, sent))
    came = lax.ppermute(sent, AXES, [(i, (i + 1) % count) for i in range(count)])
    grams = lax.all_to_all(grams, AXES, 0, 0, tiled=True)
    adjoint, factors = finish(grams, field_d, field_w)
    return (adjoint, blend(factors, own, came))


def solution(mesh):
    in_specs = (
        P(None, AXES),
        P(AXES),
        P(AXES, None, None),
        P(AXES, None),
        P(AXES, None),
        P(AXES, None),
    )
    out_specs = (P(None, AXES), P(None, AXES))
    return jax.shard_map(
        on_device, mesh=mesh, in_specs=in_specs, out_specs=out_specs, check_vma=False
    )
```

```python
import functools

import jax
import jax.numpy as jnp
from jax import lax
from jax.experimental import pallas as pl
from jax.experimental.pallas import tpu as pltpu
from jax.sharding import PartitionSpec as P

AXES = ("gx", "gy", "gz")
F32 = jnp.float32
BF16 = jnp.bfloat16
NT = (((1,), (1,)), ((), ()))
VMEM_LIMIT = 16 * 1024 * 1024

NBLK = 64
BDOF = 64
OUTS = 16
FACE = 16
HALF = FACE // 2
EXTB = NBLK + 6 * FACE
COUPLED = 7
PAIRS = 4
WIDE = PAIRS * 2 * BDOF
DEPTH = 8
STEPS = NBLK // DEPTH
TILES = BDOF // 2
GROUP = 32
ROW_STRIDE = 3
BLOCK_STRIDE = ROW_STRIDE * TILES + 1
ZONE_DEV = 128
WINDOW = 2 * ZONE_DEV


def spec_smem():
    return pl.BlockSpec(memory_space=pltpu.SMEM)


def spec_full(shape):
    return pl.BlockSpec(shape, lambda *_: (0,) * len(shape))


def spec_vmem():
    return pl.BlockSpec(memory_space=pltpu.VMEM)


def in_vmem(value):
    return pltpu.with_memory_space_constraint(value, pltpu.VMEM)


def all_in_vmem(values):
    return [in_vmem(value) for value in values]


def in_hbm(value):
    return pltpu.with_memory_space_constraint(value, pltpu.HBM)


def params(flops, moved):
    return dict(
        compiler_params=pltpu.CompilerParams(vmem_limit_bytes=VMEM_LIMIT),
        cost_estimate=pl.CostEstimate(flops=flops, bytes_accessed=moved, transcendentals=0),
    )


def lanes(shape):
    return lax.broadcasted_iota(jnp.int32, shape, len(shape) - 1)


def low_half(shape):
    return lanes(shape) < BDOF


def swap_halves(value):
    return pltpu.roll(value, BDOF, value.ndim - 1)


def split_pair(tile):
    low = low_half(tile.shape)
    other = swap_halves(tile)
    return jnp.where(low, tile, other), jnp.where(low, other, tile)


def join_pair(first, second):
    return jnp.where(low_half(first.shape), first, second)


def high_low(value):
    high = value.astype(BF16)
    low = (value - high.astype(F32)).astype(BF16)
    return jnp.concatenate([high, low], axis=0)


def fold_rows(value):
    half = value.shape[0] // 2
    return value[:half] + value[half:]


def interleave(value, back=False):
    high = value.astype(BF16).astype(F32)
    rest = value - high
    middle = rest.astype(BF16).astype(F32)
    lowest = rest - middle
    low = low_half(value.shape)
    parts = jnp.concatenate([jnp.where(low, high, middle), lowest], axis=1).astype(BF16)
    source = lax.broadcasted_iota(jnp.int32, (4 * BDOF, 2 * BDOF), 0)
    target = lanes((4 * BDOF, 2 * BDOF)) % BDOF
    within = source % BDOF
    halved, whole = (target, within) if back else (within, target)
    place = (halved % (BDOF // 2)) * 2 + halved // (BDOF // 2)
    mover = jnp.where((place == whole) & (source < 3 * BDOF), 1.0, 0.0).astype(BF16)
    return jnp.dot(parts, mover, preferred_element_type=F32)


def slots_of(sizes):
    order = []
    for axis in (2, 0, 1):
        for turn in (0, 1) if axis == 2 else (1, 0):
            if sizes[axis] > 1 + turn:
                order.append((axis, turn))
    return order


def side_of(slot):
    axis, turn = slot
    odd = lax.axis_index(AXES[axis]) % 2
    return 2 * axis + (odd if turn else 1 - odd)


def partner_exists(slot, sizes):
    axis, turn = slot
    place = lax.axis_index(AXES[axis])
    partner = place + 2 * (side_of(slot) % 2) - 1
    return (partner >= 0) & (partner < sizes[axis])


def start_kernel(slots, face_ref, loads_ref, disp_ref, stiff_ref, dirs_ref, inv_ref, *rest):
    msgs, (udup_ref,) = rest[:-1], rest[-1:]
    lane = lanes((DEPTH, 2 * BDOF))
    for step in range(STEPS):
        rows = slice(step * DEPTH, (step + 1) * DEPTH)
        parts = []
        for tile in range(TILES):
            part = stiff_ref[0, rows, tile * 128:(tile + 1) * 128]
            parts.append(jnp.where((lane == 2 * tile) | (lane == BDOF + 2 * tile + 1), part, 0.0))
        while len(parts) > 1:
            parts = [one + two for one, two in zip(parts[::2], parts[1::2])]
        inv_ref[rows, :] = 1.0 / (parts[0] + swap_halves(parts[0]))
    for pair in range(NBLK // 2):
        first, second = split_pair(loads_ref[:, pair * 128:(pair + 1) * 128])
        dirs_ref[2 * pair] = first * inv_ref[2 * pair:2 * pair + 1, :]
        dirs_ref[2 * pair + 1] = second * inv_ref[2 * pair + 1:2 * pair + 2, :]
    one, two = split_pair(disp_ref[...])
    udup_ref[pl.ds(0, NBLK // 2, stride=2), :] = one
    udup_ref[pl.ds(1, NBLK // 2, stride=2), :] = two
    for msg, slot in zip(msgs, slots):
        side = side_of(slot)
        for pair in range(HALF):
            one, two = face_ref[side, 2 * pair], face_ref[side, 2 * pair + 1]
            msg[pair * OUTS:(pair + 1) * OUTS, :] = join_pair(dirs_ref[one], dirs_ref[two])
            msg[HALF * OUTS + pair:HALF * OUTS + pair + 1, :] = join_pair(
                udup_ref[pl.ds(one, 1), :], udup_ref[pl.ds(two, 1), :]
            )


def start(slots, face_index, loads, disp, stiffness):
    msg_rows = HALF * (OUTS + 1)
    outs = [pltpu.VMEM((NBLK, OUTS, 2 * BDOF), F32), pltpu.VMEM((NBLK, 2 * BDOF), F32)]
    outs += [jax.ShapeDtypeStruct((msg_rows, 2 * BDOF), F32)] * len(slots)
    return pl.pallas_call(
        functools.partial(start_kernel, slots),
        grid=(1,),
        in_specs=[
            spec_smem(),
            spec_full(loads.shape),
            spec_full(disp.shape),
            pl.BlockSpec((1, NBLK, BDOF * BDOF), lambda s: (0, 0, 0)),
        ],
        out_specs=[spec_vmem()] * 2 + [spec_full(o.shape) for o in outs[2:]],
        out_shape=outs,
        scratch_shapes=[pltpu.VMEM((NBLK, 2 * BDOF), F32)],
        name="start",
        **params(1 << 20, 2 << 20),
    )(in_hbm(face_index), in_hbm(loads), in_hbm(disp), in_hbm(stiffness))


def pack_kernel(stiff_ref, out_ref, rows_ref):
    span = DEPTH * BLOCK_STRIDE

    def chunk(step, carry):
        own = pl.ds(pl.multiple_of(step * DEPTH, DEPTH), DEPTH)
        for side in range(COUPLED):
            for tile in range(TILES):
                rows_ref[pl.ds(side * span + tile * ROW_STRIDE, DEPTH, stride=BLOCK_STRIDE), :] = stiff_ref[
                    side, own, tile * 128:(tile + 1) * 128
                ]

        def matrix(side, row):
            return rows_ref[pl.ds(side * span + row * BLOCK_STRIDE, TILES, stride=ROW_STRIDE), :]

        for row in range(DEPTH):
            at = step * DEPTH + row
            for pair in range(PAIRS):
                first = matrix(2 * pair, row)
                second = matrix(2 * pair + 1, row) if 2 * pair + 1 < COUPLED else jnp.zeros_like(first)
                low = low_half(first.shape)
                even = jnp.where(low, first, swap_halves(second))
                odd = jnp.where(low, swap_halves(first), second)
                both = jnp.concatenate([even, odd], axis=0)
                out_ref[at, :, pair * 128:(pair + 1) * 128] = high_low(both)
        return carry

    lax.fori_loop(0, STEPS, chunk, 0)


def pack(stiffness):
    return pl.pallas_call(
        pack_kernel,
        in_specs=[spec_vmem()],
        out_specs=spec_vmem(),
        out_shape=pltpu.VMEM((NBLK, 2 * BDOF, WIDE), BF16),
        scratch_shapes=[
            pltpu.VMEM((COUPLED * DEPTH * BLOCK_STRIDE + 8, 2 * BDOF), F32),
        ],
        name="pack",
        **params(1 << 24, 16 << 20),
    )(in_vmem(stiffness))


def two_parts(value):
    high = value.astype(BF16)
    return high, (value - high.astype(F32)).astype(BF16)


def fill_halos(store, slots, sizes, halos, first_row, rows):
    met = set()
    for slot, halo in zip(slots, halos):
        side = side_of(slot)
        met.add(slot)
        exists = None
        if slot[1] == 1 or sizes[slot[0]] % 2 == 1:
            exists = partner_exists(slot, sizes)
        for pair in range(HALF):
            at = NBLK + side * FACE + 2 * pair
            for extra, value in enumerate(split_pair(halo[first_row + pair * rows:first_row + (pair + 1) * rows, :])):
                store(at + extra, value if exists is None else jnp.where(exists, value, 0.0))
    for axis in range(3):
        for turn in range(2):
            if (axis, turn) not in met:
                side = side_of((axis, turn))
                for block in range(FACE):
                    store(NBLK + side * FACE + block, jnp.zeros((rows, 2 * BDOF), F32))


def fill_extended(slots, sizes, ext_ref, own_ref, halos):
    for block in range(NBLK):
        ext_ref[block] = high_low(own_ref[block])

    def store(at, value):
        ext_ref[at] = high_low(value)

    fill_halos(store, slots, sizes, halos, 0, OUTS)


def gathered(ext_ref, col_ref, row):
    pieces = []
    for pair in range(PAIRS):
        first = ext_ref[col_ref[2 * pair, row]]
        if 2 * pair + 1 < COUPLED:
            pieces.append(join_pair(first, ext_ref[col_ref[2 * pair + 1, row]]))
        else:
            pieces.append(join_pair(first, jnp.zeros_like(first)))
    return jnp.concatenate(pieces, axis=1)


def times_packed(field, packed):
    out = fold_rows(lax.dot_general(field, packed, NT, preferred_element_type=F32))
    return out + swap_halves(out)


def operate(col_ref, packed_ref, ext_ref, image_ref):
    def chunk(step, carry):
        for local in range(GROUP):
            row = step * GROUP + local
            at = pl.multiple_of(row * OUTS, OUTS)
            image_ref[pl.ds(at, OUTS), :] = times_packed(gathered(ext_ref, col_ref, row), packed_ref[row])
        return carry

    lax.fori_loop(0, NBLK // GROUP, chunk, 0)


def first_kernel(slots, sizes, col_ref, face_ref, packed_ref, dirs_ref, inv_ref, loads_ref, *rest):
    many = len(slots)
    halos, (w_ref, turn_ref, gram_ref), msgs = rest[:many], rest[many:many + 3], rest[many + 3:2 * many + 3]
    ext_ref, image_ref, left_ref, right_ref = rest[2 * many + 3:]
    fill_extended(slots, sizes, ext_ref, dirs_ref, halos)
    operate(col_ref, packed_ref, ext_ref, image_ref)
    inv_turned = interleave(inv_ref[...], True)
    for block in range(NBLK):
        turn_ref[block] = image_ref[block * OUTS:(block + 1) * OUTS, :] * inv_turned[block:block + 1, :]
    image = interleave(image_ref[...])
    for pair in range(NBLK // 2):
        one = image[2 * pair * OUTS:(2 * pair + 1) * OUTS]
        two = image[(2 * pair + 1) * OUTS:(2 * pair + 2) * OUTS]
        w_one = one * inv_ref[2 * pair:2 * pair + 1, :]
        w_two = two * inv_ref[2 * pair + 1:2 * pair + 2, :]
        w_ref[2 * pair] = w_one
        w_ref[2 * pair + 1] = w_two
        at = slice(pair * 128, (pair + 1) * 128)
        own = join_pair(dirs_ref[2 * pair], dirs_ref[2 * pair + 1])
        left_ref[:, at] = high_low(
            jnp.concatenate([loads_ref[:, at], own, join_pair(w_one, w_two)], axis=0)
        )
        right_ref[:, at] = high_low(jnp.concatenate([own, join_pair(one, two)], axis=0))
    for msg, slot in zip(msgs, slots):
        side = side_of(slot)
        for pair in range(HALF):
            msg[pair * OUTS:(pair + 1) * OUTS, :] = join_pair(
                w_ref[face_ref[side, 2 * pair]], w_ref[face_ref[side, 2 * pair + 1]]
            )
    gram = fold_rows(lax.dot_general(left_ref[...], right_ref[...], NT, preferred_element_type=F32))
    gram = gram[:, :2 * OUTS] + gram[:, 2 * OUTS:]
    gram_ref[...] = jnp.concatenate(
        [gram[:OUTS, :OUTS], gram[OUTS:2 * OUTS, OUTS:], gram[2 * OUTS:, OUTS:]], axis=1
    )


def first(slots, sizes, col_index, face_index, packed, dirs, inv, loads, halos):
    outs = [
        pltpu.VMEM((NBLK, OUTS, 2 * BDOF), F32),
        pltpu.VMEM((NBLK, OUTS, 2 * BDOF), F32),
        pltpu.VMEM((OUTS, 3 * OUTS), F32),
    ] + [jax.ShapeDtypeStruct((HALF * OUTS, 2 * BDOF), F32)] * len(slots)
    return pl.pallas_call(
        functools.partial(first_kernel, slots, sizes),
        in_specs=[
            spec_smem(),
            spec_smem(),
        ] + [spec_vmem()] * (4 + len(halos)),
        out_specs=[spec_vmem()] * 3 + [spec_full(o.shape) for o in outs[3:]],
        out_shape=outs,
        scratch_shapes=[
            pltpu.VMEM((EXTB, 2 * OUTS, 2 * BDOF), BF16),
            pltpu.VMEM((NBLK * OUTS, 2 * BDOF), F32),
            pltpu.VMEM((6 * OUTS, NBLK * BDOF), BF16),
            pltpu.VMEM((4 * OUTS, NBLK * BDOF), BF16),
        ],
        name="first",
        **params(1 << 28, 11 << 20),
    )(col_index, face_index, *all_in_vmem((packed, dirs, inv, loads, *halos)))


def inner_kernel(slots, sizes, col_ref, packed_ref, w_ref, disp_ref, *rest):
    many = len(slots)
    halos, (image_ref, raw_ref, ext_ref, udup_ref, near_ref) = rest[:many], rest[many:]
    for block in range(NBLK):
        ext_ref[block] = high_low(w_ref[block])
    for block in range(NBLK, EXTB):
        ext_ref[block] = jnp.zeros((2 * OUTS, 2 * BDOF), BF16)
    one, two = split_pair(disp_ref[...])
    udup_ref[pl.ds(0, NBLK // 2, stride=2), :] = one
    udup_ref[pl.ds(1, NBLK // 2, stride=2), :] = two

    def store(at, value):
        udup_ref[pl.ds(at, 1), :] = value

    fill_halos(store, slots, sizes, halos, HALF * OUTS, 1)
    side_at = lax.broadcasted_iota(jnp.int32, (8, 128), 0)
    low = low_half((8, 128))

    def chunk(step, carry):
        for local in range(GROUP):
            row = step * GROUP + local
            own = udup_ref[pl.ds(row, 1), :]
            for side in range(COUPLED):
                near_ref[local * 8 + side:local * 8 + side + 1, :] = udup_ref[pl.ds(col_ref[side, row], 1), :]
            near_ref[local * 8 + 7:local * 8 + 8, :] = own
            differ = own - near_ref[local * 8:(local + 1) * 8, :]
            parts = []
            for pair in range(PAIRS):
                keep = ((side_at == 2 * pair) & low) | ((side_at == 2 * pair + 1) & ~low)
                part = jnp.where(keep, differ, 0.0)
                high = part.astype(BF16).astype(F32)
                parts.append(jnp.concatenate([high, part - high], axis=0).astype(BF16))
            field = jnp.concatenate([gathered(ext_ref, col_ref, row), jnp.concatenate(parts, axis=1)], axis=0)
            out = lax.dot_general(field, packed_ref[row], NT, preferred_element_type=F32)
            both = jnp.concatenate([fold_rows(out[:2 * OUTS]), fold_rows(out[2 * OUTS:])], axis=0)
            both = both + swap_halves(both)
            image_ref[pl.ds(pl.multiple_of(row * OUTS, OUTS), OUTS), :] = both[:OUTS]
            raw_ref[pl.ds(pl.multiple_of(row * 8, 8), 8), :] = both[OUTS:]
        return carry

    lax.fori_loop(0, NBLK // GROUP, chunk, 0)


def inner(slots, sizes, col_index, packed, w, disp, halos):
    return pl.pallas_call(
        functools.partial(inner_kernel, slots, sizes),
        in_specs=[spec_smem()] + [spec_vmem()] * (3 + len(halos)),
        out_specs=[spec_vmem()] * 2,
        out_shape=[pltpu.VMEM((NBLK * OUTS, 128), F32), pltpu.VMEM((NBLK * 8, 128), F32)],
        scratch_shapes=[
            pltpu.VMEM((EXTB, 2 * OUTS, 2 * BDOF), BF16),
            pltpu.VMEM((EXTB, 2 * BDOF), F32),
            pltpu.VMEM((GROUP * 8, 2 * BDOF), F32),
        ],
        name="inner",
        **params(1 << 28, 10 << 20),
    )(col_index, *all_in_vmem((packed, w, disp, *halos)))


def outer_kernel(slots, sizes, face_ref, packed_ref, w_ref, early_ref, inner_ref, *rest):
    many = len(slots)
    halos, (gram_ref, image_ref, left_ref, right_ref) = rest[:many], rest[many:]
    image_ref[...] = inner_ref[...]
    half_at = lanes((OUTS, 2 * BDOF)) // BDOF
    for slot, halo in zip(slots, halos):
        side = side_of(slot)
        upper = side % 2
        pair_at = pl.multiple_of((slot[0] + upper) * 128, 128)
        keep = half_at == 1 - upper
        if slot[1] == 1 or sizes[slot[0]] % 2 == 1:
            keep = keep & partner_exists(slot, sizes)
        for pair in range(HALF):
            for extra, value in enumerate(split_pair(halo[pair * OUTS:(pair + 1) * OUTS, :])):
                row = face_ref[side, 2 * pair + extra]
                field = high_low(jnp.where(keep, value, 0.0))
                at = pl.ds(pl.multiple_of(row * OUTS, OUTS), OUTS)
                image_ref[at, :] += times_packed(field, packed_ref[row, :, pl.ds(pair_at, 128)])
    for pair in range(NBLK // 2):
        one = image_ref[2 * pair * OUTS:(2 * pair + 1) * OUTS, :]
        two = image_ref[(2 * pair + 1) * OUTS:(2 * pair + 2) * OUTS, :]
        at = slice(pair * 128, (pair + 1) * 128)
        left_ref[:, at] = high_low(join_pair(w_ref[2 * pair], w_ref[2 * pair + 1]))
        right_ref[:, at] = high_low(join_pair(one, two))
    gram = fold_rows(lax.dot_general(left_ref[...], right_ref[...], NT, preferred_element_type=F32))
    grams = jnp.concatenate([gram[:, :OUTS] + gram[:, OUTS:], early_ref[...]], axis=1)
    tile = jnp.concatenate([grams[:8], grams[8:]], axis=1)
    for place in range(gram_ref.shape[0] // 8):
        gram_ref[place * 8:(place + 1) * 8, :] = tile


def outer(slots, sizes, face_index, packed, w, early, image, halos):
    copies = sizes[0] * sizes[1] * sizes[2]
    return pl.pallas_call(
        functools.partial(outer_kernel, slots, sizes),
        in_specs=[spec_smem()] + [spec_vmem()] * (4 + len(halos)),
        out_specs=spec_full((copies * 8, 128)),
        out_shape=jax.ShapeDtypeStruct((copies * 8, 128), F32),
        scratch_shapes=[
            pltpu.VMEM((NBLK * OUTS, 2 * BDOF), F32),
            pltpu.VMEM((2 * OUTS, NBLK * BDOF), BF16),
            pltpu.VMEM((2 * OUTS, NBLK * BDOF), BF16),
        ],
        name="outer",
        **params(1 << 27, 4 << 20),
    )(face_index, *all_in_vmem((packed, w, early, image, *halos)))


def terms_kernel(slots, sizes, col_ref, moved_ref, zone_ref, dirs_ref, w_ref, *rest):
    many = len(slots)
    halos_d, halos_w = rest[:many], rest[many:2 * many]
    own_ref, sent_ref, field_d_ref, field_w_ref, ext_d, ext_w, term_ref, value_ref = rest[2 * many:]
    value_ref[...] = interleave(moved_ref[...])
    fill_extended(slots, sizes, ext_d, dirs_ref, halos_d)
    fill_extended(slots, sizes, ext_w, w_ref, halos_w)
    for ext_ref, field_ref in ((ext_d, field_d_ref), (ext_w, field_w_ref)):
        for pair in range(NBLK // 2):
            field_ref[:, pair * 128:(pair + 1) * 128] = join_pair(ext_ref[2 * pair], ext_ref[2 * pair + 1])
    side_at = lax.broadcasted_iota(jnp.int32, (8, 128), 0)
    low = low_half((8, 128))

    def chunk(step, carry):
        for local in range(GROUP):
            row = step * GROUP + local
            at = pl.multiple_of(row * 8, 8)
            value = value_ref[pl.ds(at, 8), :]
            pieces = []
            for pair in range(PAIRS):
                drop = ((side_at == 2 * pair) & low) | ((side_at == 2 * pair + 1) & ~low)
                part = jnp.where(drop, -value, 0.0)
                if pair == 0:
                    part = jnp.where(low, value, part)
                high = part.astype(BF16).astype(F32)
                pieces.append(jnp.concatenate([high, part - high], axis=0).astype(BF16))
            fields = jnp.concatenate([gathered(ext_d, col_ref, row), gathered(ext_w, col_ref, row)], axis=0)
            out = lax.dot_general(
                jnp.concatenate(pieces, axis=1), fields, NT, preferred_element_type=F32
            )
            term_ref[pl.ds(at, 8), :4 * OUTS] = fold_rows(out)
        return carry

    lax.fori_loop(0, NBLK // GROUP, chunk, 0)
    across = jnp.concatenate([term_ref[pl.ds(side, NBLK, stride=8), :] for side in range(1, COUPLED)], axis=0)
    term = jnp.transpose(across)
    term = jnp.concatenate([fold_rows(term[:2 * OUTS]), fold_rows(term[2 * OUTS:4 * OUTS])], axis=0)
    high = term.astype(BF16)
    rest_of = term - high.astype(F32)
    middle = rest_of.astype(BF16)
    stack = jnp.concatenate([high, middle, (rest_of - middle.astype(F32)).astype(BF16)], axis=0)
    me = (lax.axis_index(AXES[0]) * sizes[1] + lax.axis_index(AXES[1])) * sizes[2] + lax.axis_index(AXES[2])
    relative = zone_ref[...] - me * ZONE_DEV
    relative = jnp.where(relative < 0, relative + ZONE_DEV * sizes[0] * sizes[1] * sizes[2], relative)
    relative = jnp.concatenate([relative[side:side + 1, :] for side in range(COUPLED - 1)], axis=1)
    place = lax.broadcasted_iota(jnp.int32, (WINDOW, NBLK * (COUPLED - 1)), 0)
    member = jnp.where(relative == place, 1.0, 0.0).astype(BF16)
    sums = lax.dot_general(stack, member, NT, preferred_element_type=F32)
    sums = sums[:2 * OUTS] + sums[2 * OUTS:4 * OUTS] + sums[4 * OUTS:]
    own_ref[...] = sums[:, :ZONE_DEV]
    sent_ref[...] = sums[:, ZONE_DEV:]


def terms(slots, sizes, col_index, values, zones, dirs, w, halos_d, halos_w):
    operands = (values, zones, dirs, w, *halos_d, *halos_w)
    outs = [jax.ShapeDtypeStruct((2 * OUTS, ZONE_DEV), F32)] * 2
    outs += [pltpu.VMEM((2 * OUTS, NBLK * BDOF), BF16)] * 2
    return pl.pallas_call(
        functools.partial(terms_kernel, slots, sizes),
        in_specs=[spec_smem()] + [spec_vmem()] * len(operands),
        out_specs=[spec_full((2 * OUTS, ZONE_DEV))] * 2 + [spec_vmem()] * 2,
        out_shape=outs,
        scratch_shapes=[
            pltpu.VMEM((EXTB, 2 * OUTS, 2 * BDOF), BF16),
            pltpu.VMEM((EXTB, 2 * OUTS, 2 * BDOF), BF16),
            pltpu.VMEM((NBLK * 8, 128), F32),
            pltpu.VMEM((NBLK * 8, 128), F32),
        ],
        name="terms",
        **params(1 << 27, 4 << 20),
    )(col_index, *all_in_vmem(operands))


def times(left, right):
    parts = [left[:, i:i + 1] * right[i:i + 1, :] for i in range(left.shape[1])]
    while len(parts) > 1:
        parts = [one + two for one, two in zip(parts[::2], parts[1::2])]
    return parts[0]


def solve_spd(matrix, right):
    work = jnp.concatenate([matrix, right], axis=1)
    rows = lax.broadcasted_iota(jnp.int32, work.shape, 0)
    for at in range(0, OUTS, 2):
        first_col = jnp.broadcast_to(work[:, at:at + 1], work.shape)
        second_col = jnp.broadcast_to(work[:, at + 1:at + 2], work.shape)
        one, two = work[at:at + 1, :], work[at + 1:at + 2, :]
        top, side, end = first_col[at:at + 1], first_col[at + 1:at + 2], second_col[at + 1:at + 2]
        scale = 1.0 / (top * end - side * side)
        new_one = (end * one - side * two) * scale
        new_two = (top * two - side * one) * scale
        others = work - first_col * new_one - second_col * new_two
        work = jnp.where(rows == at, new_one, jnp.where(rows == at + 1, new_two, others))
    return work[:, OUTS:]


def finish_kernel(grams_ref, dirs_ref, w_ref, adj_ref, factors_ref):
    count = grams_ref.shape[0] // 8
    parts = [grams_ref[i * 8:(i + 1) * 8, :] for i in range(count)]
    while len(parts) > 1:
        parts = [sum(parts[i:i + 2][1:], parts[i]) for i in range(0, len(parts), 2)]
    gram = jnp.concatenate([parts[0][:, :4 * OUTS], parts[0][:, 4 * OUTS:]], axis=0)
    f_gram = gram[:, :OUTS]
    n_gram = gram[:, OUTS:2 * OUTS]
    c_gram = gram[:, 2 * OUTS:3 * OUTS]
    e_gram = gram[:, 3 * OUTS:]
    eye = jnp.where(
        lax.broadcasted_iota(jnp.int32, (OUTS, OUTS), 0) == lanes((OUTS, OUTS)), 1.0, 0.0
    )
    n_inverse = solve_spd(n_gram, eye)
    alpha = solve_spd(c_gram, n_gram)
    alpha_t = jnp.transpose(alpha)
    c_alpha = times(c_gram, alpha)
    e_alpha = times(e_gram, alpha)
    f_alpha = times(f_gram, alpha)
    next_gram = n_gram - c_alpha - jnp.transpose(c_alpha) + times(alpha_t, e_alpha)
    mixed = eye + times(n_inverse, next_gram)
    mixed_t = jnp.transpose(mixed)
    cross = times(mixed_t, e_alpha)
    curvature = times(mixed_t, times(c_gram, mixed)) - cross - jnp.transpose(cross) + times(alpha_t, f_alpha)
    beta_t = jnp.transpose(solve_spd(curvature, next_gram))
    on_dirs = alpha_t + times(beta_t, mixed_t)
    on_w = -times(beta_t, alpha_t)
    factors = jnp.concatenate([on_dirs, on_w], axis=1)
    high, low = two_parts(factors)
    factors_split = [high[:, :OUTS], high[:, :OUTS], high[:, OUTS:], high[:, OUTS:], low]
    dirs, w = dirs_ref[...], w_ref[...]
    adj_ref[...] = jnp.dot(
        jnp.concatenate(factors_split, axis=1),
        jnp.concatenate([dirs, w, dirs[:OUTS], w[:OUTS]], axis=0),
        preferred_element_type=F32,
    )
    factors_ref[...] = factors


def blend_kernel(factors_ref, own_ref, came_ref, sens_ref):
    sens_ref[...] = 0.5 * jnp.dot(
        factors_ref[...], own_ref[...] + came_ref[...], precision=lax.Precision.HIGHEST, preferred_element_type=F32
    )


def finish(grams, dirs, w):
    operands = (grams, dirs, w)
    outs = [
        jax.ShapeDtypeStruct((OUTS, NBLK * BDOF), F32),
        jax.ShapeDtypeStruct((OUTS, 2 * OUTS), F32),
    ]
    return pl.pallas_call(
        finish_kernel,
        in_specs=[spec_vmem()] * 3,
        out_specs=[spec_full(o.shape) for o in outs],
        out_shape=outs,
        name="finish",
        **params(1 << 25, 8 << 20),
    )(*all_in_vmem(operands))


def blend(factors, own, came):
    operands = (factors, own, came)
    return pl.pallas_call(
        blend_kernel,
        in_specs=[spec_full(o.shape) for o in operands],
        out_specs=spec_full((OUTS, ZONE_DEV)),
        out_shape=jax.ShapeDtypeStruct((OUTS, ZONE_DEV), F32),
        name="blend",
        **params(1 << 17, 1 << 16),
    )(*operands)


def exchange(slots, msgs):
    halos = []
    for (axis, turn), msg in zip(slots, msgs):
        count = lax.axis_size(AXES[axis])
        pairs = []
        for place in range(count):
            partner = place + 1 if place % 2 == turn else place - 1
            pairs.append((place, partner if 0 <= partner < count else place))
        halos.append(lax.ppermute(msg, AXES[axis], pairs))
    return halos


def on_device(loads, displacement, stiffness, col_index, face_index, zone_map):
    sizes = [lax.axis_size(axis) for axis in AXES]
    slots = slots_of(sizes)
    disp = displacement.reshape(NBLK // 2, 2 * BDOF)
    stiffness = jnp.swapaxes(stiffness, 0, 1)
    col_index = col_index.T
    dirs, inv, *msgs = start(slots, face_index, loads, disp, stiffness)
    halos_d = exchange(slots, msgs)
    packed = pack(stiffness)
    w, w_turned, early, *msgs = first(slots, sizes, col_index, face_index, packed, dirs, inv, loads, halos_d)
    halos_w = exchange(slots, msgs)
    image, values = inner(slots, sizes, col_index, packed, w, disp, halos_d)
    count = lax.axis_size(AXES)
    zones = zone_map.T
    grams = outer(slots, sizes, face_index, packed, w_turned, early, image, halos_w)
    own, sent, field_d, field_w = terms(slots, sizes, col_index, values, zones, dirs, w, halos_d, halos_w)
    came = lax.ppermute(sent, AXES, [(i, (i + 1) % count) for i in range(count)])
    grams = lax.all_to_all(grams, AXES, 0, 0, tiled=True)
    adjoint, factors = finish(grams, field_d, field_w)
    return (adjoint, blend(factors, own, came))


def solution(mesh):
    in_specs = (
        P(None, AXES),
        P(AXES),
        P(AXES, None, None),
        P(AXES, None),
        P(AXES, None),
        P(AXES, None),
    )
    out_specs = (P(None, AXES), P(None, AXES))
    return jax.shard_map(
        on_device, mesh=mesh, in_specs=in_specs, out_specs=out_specs, check_vma=False
    )
```
